512 devices in a mesh: grp: 128 (over z, y, core), col: 4 (over x).
Axes of the slice: x: 4, y: 8, z: 8, core: 2. Of those that a mesh axis runs over, the one named last changes fastest.
Arguments:
- points: float32 [65536, 1024], P(('grp', 'col')), may hold values from -1000 to 1000
- labels: int32 [65536], P(('grp', 'col')), may hold values from 0 to 31, as said below
- boundaries: int32 [33], replicated, may hold values from 0 to 128, as said below
- centroids: float32 [128, 512, 1024], P('grp', 'col'), may hold values from -12 to 12, as said below
Outputs:
- centroid_table: float32 [128, 512, 1024], P('grp', 'col')
The draws below stay inside these ranges and needn't reach their ends.
Inputs may be any that keep to these rules, and one draw needn't show every extreme that they name: `labels`: on each device's rows, the rows that name parent p number at most 2 times the number of grp indices in p's group; on every device some parent reaches this. boundaries[0] = 0 and boundaries[32] = 128; every group has 1 to 7 grp indices, and some group has 7. `centroids`: rows of the table at grp indices of one parent's group are equal.
All inputs are finite; a program needn't handle non-finite values.
Results may differ from the reference program's by a relative error of at most 0.0003.
Values sent between devices are 32-bit elements; how exact they have to be, the bound alone decides.
A program may use at most 64 MiB of HBM per device.

```python
import jax
import jax.numpy as jnp
from jax import lax

D = 1024
K = 512
ITERS = 2
ROWS_DEV = 128
PARENTS = 32
CAP = 2
TOKENS = 65536
N_GRP = 128
N_COL = 4


def group_bounds(key):
    local_key = jax.random.fold_in(key, 101)
    first_key, second_key = jax.random.split(local_key)
    extras = jax.random.randint(first_key, (PARENTS // 2,), 0, 7)
    extras = extras.at[0].set(0)
    paired = jnp.stack([1 + extras, 7 - extras], axis=1).reshape(PARENTS)
    shuffle = jax.random.permutation(second_key, PARENTS)
    group_sizes = paired[shuffle].astype(jnp.int32)
    bounds = jnp.concatenate([jnp.zeros((1,), jnp.int32), jnp.cumsum(group_sizes).astype(jnp.int32)])
    return (bounds, group_sizes)


def device_owner(bounds):
    devices = jnp.arange(N_GRP, dtype=jnp.int32)
    return jnp.sum((bounds[1:][None, :] <= devices[:, None]).astype(jnp.int32), axis=1).astype(jnp.int32)


def child_base(key):
    return jax.random.normal(jax.random.fold_in(key, 202), (PARENTS, K, D), jnp.float32)


def all_labels(key):
    bounds, group_sizes = group_bounds(key)
    owners = device_owner(bounds)
    seat_count = N_GRP * CAP
    seat_parent = owners[jnp.arange(seat_count, dtype=jnp.int32) // CAP]
    label_key = jax.random.fold_in(key, 303)

    def one_shard(shard):
        shard_key = jax.random.fold_in(label_key, shard)
        key_list = jax.random.split(shard_key, 3)
        priority = jax.random.permutation(key_list[0], seat_count).astype(jnp.int32)
        ranking = jax.random.permutation(key_list[1], PARENTS).astype(jnp.int32)
        eligible = jnp.where(group_sizes * CAP <= ROWS_DEV, ranking, PARENTS + ranking)
        favored = jnp.argmin(eligible).astype(jnp.int32)
        scores = priority + jnp.where(seat_parent == favored, 0, seat_count).astype(jnp.int32)
        negated, picked = lax.top_k(-scores, ROWS_DEV)
        chosen = seat_parent[picked]
        return chosen[jax.random.permutation(key_list[2], ROWS_DEV)]
    shards = jax.vmap(one_shard)(jnp.arange(N_GRP * N_COL, dtype=jnp.int32))
    return shards.reshape(TOKENS).astype(jnp.int32)


def draw_labels(key, part):
    shared = all_labels(key)
    return shared


def draw_boundaries(key, part):
    bounds, group_sizes = group_bounds(key)
    return bounds


def draw_centroids(key, part):
    bounds, group_sizes = group_bounds(key)
    base = child_base(key)
    key = jax.random.fold_in(key, 5)
    guessed = base + 0.5 * jax.random.normal(key, base.shape, jnp.float32)
    return guessed[device_owner(bounds)]


def draw_points(key, part):
    labels = all_labels(key)
    base = child_base(key)
    key = jax.random.fold_in(key, 6)
    key_list = jax.random.split(key, 2)
    child = jax.random.randint(key_list[0], (TOKENS,), 0, K)
    centers = base[labels, child]
    return centers + jax.random.normal(key_list[1], (TOKENS, D), jnp.float32)


def setup_inputs(seed: int = 0) -> dict:
    arg_keys = jax.random.split(jax.random.key(seed), 5)
    return {
        "points": draw_points(jax.random.fold_in(arg_keys[4], 71), 0),
        "labels": draw_labels(jax.random.fold_in(arg_keys[4], 71), 0),
        "boundaries": draw_boundaries(jax.random.fold_in(arg_keys[4], 71), 0),
        "centroids": draw_centroids(jax.random.fold_in(arg_keys[4], 71), 0),
    }


SHARPNESS = 6.0
HIGHEST = lax.Precision.HIGHEST


def reference(points, labels, boundaries, centroids):
    block = 512
    row_total = points.shape[0]
    parent_ids = jnp.arange(PARENTS, dtype=jnp.int32)
    member = (labels[:, None] == parent_ids[None, :]).astype(jnp.int32)
    counts = jnp.sum(member, axis=0).astype(jnp.int32)
    sorted_order = jnp.argsort(labels, stable=True)
    ordered = jnp.concatenate([points[sorted_order], jnp.zeros((block, D), points.dtype)], axis=0)
    zero_one = jnp.zeros((1,), jnp.int32)
    starts = jnp.concatenate([zero_one, jnp.cumsum(counts).astype(jnp.int32)])
    block_counts = ((counts + block - 1) // block).astype(jnp.int32)
    block_starts = jnp.concatenate([zero_one, jnp.cumsum(block_counts).astype(jnp.int32)])
    block_total = row_total // block + PARENTS
    score_scale = SHARPNESS / D
    current = centroids[boundaries[:-1]]
    for iteration in range(ITERS):
        half_norm = 0.5 * jnp.sum(current * current, axis=2)

        def visit(state_pair, block_index):
            weighted, mass_sum = state_pair
            owner_id = jnp.minimum(jnp.sum((block_starts[1:] <= block_index).astype(jnp.int32)), PARENTS - 1).astype(jnp.int32)
            inner_row = ((block_index - block_starts[owner_id]) * block).astype(jnp.int32)
            offset = (starts[owner_id] + inner_row).astype(jnp.int32)
            row_block = lax.dynamic_slice_in_dim(ordered, offset, block, 0)
            is_valid = ((jnp.arange(block, dtype=jnp.int32) + inner_row) < counts[owner_id]) & (block_index < block_starts[PARENTS])
            centre = current[owner_id]
            logits = (jnp.dot(row_block, centre.T, precision=HIGHEST) - half_norm[owner_id][None, :]) * score_scale
            peak_value = jnp.max(logits, axis=1, keepdims=True)
            raised = jnp.exp(logits - peak_value)
            shares = raised * (is_valid.astype(raised.dtype) / jnp.sum(raised, axis=1))[:, None]
            added_rows = jnp.dot(shares.T, row_block, precision=HIGHEST)
            zero_index = jnp.zeros((), jnp.int32)
            weighted = lax.dynamic_update_slice(weighted, (weighted[owner_id] + added_rows)[None], (owner_id, zero_index, zero_index))
            mass_sum = lax.dynamic_update_slice(mass_sum, (mass_sum[owner_id] + jnp.sum(shares, axis=0))[None], (owner_id, zero_index))
            return (weighted, mass_sum), None

        initial = (jnp.zeros_like(current), jnp.zeros(current.shape[:2], current.dtype))
        (weighted, mass_sum), unused = lax.scan(visit, initial, jnp.arange(block_total, dtype=jnp.int32))
        current = (weighted + current) / (mass_sum + 1.0)[:, :, None]
    devices = jnp.arange(N_GRP, dtype=jnp.int32)
    owners = jnp.sum((boundaries[1:][None, :] <= devices[:, None]).astype(jnp.int32), axis=1).astype(jnp.int32)
    return current[owners]
```

```python
import functools

import jax
import jax.numpy as jnp
from jax import lax
from jax.experimental import pallas as pl
from jax.experimental.pallas import tpu as pltpu
from jax.sharding import PartitionSpec as P

ITERS = 2
SHARPNESS = 6.0
HIGHEST = lax.Precision.HIGHEST
MESH = pl.DeviceIdType.MESH
LANES = 128
SEATS = 2
MARK = 4096.0
ROUNDS = 3
WINDOW = 3
CHUNK = 256
F32 = jnp.float32
BF16 = jnp.bfloat16


def plane_shape(groups):
    chips = groups // 2
    side = 1
    while side * side < chips:
        side *= 2
    return chips // side, side


def peer(me, offset, shape):
    nz, ny = shape
    core, y, z = me % 2, (me // 2) % ny, me // (2 * ny)
    k, dz, dc = offset // (2 * nz), (offset // 2) % nz, offset % 2
    dy = (k + dz) % ny
    return (((z + dz) % nz) * ny + (y + dy) % ny) * 2 + (core + dc) % 2


def halves(x):
    hi = x.astype(BF16)
    return hi, (x - hi.astype(F32)).astype(BF16)


def dot_nt(a, b):
    return lax.dot_general(a, b, (((1,), (1,)), ((), ())), preferred_element_type=F32)


def dot_nn(a, b):
    return lax.dot_general(a, b, (((1,), (0,)), ((), ())), preferred_element_type=F32)


def kernel(
    groups, cols, bounds_ref, labels_ref, points_ref, cent_ref, out_ref,
    seats_ref, rows_ref, xh_ref, xl_ref, logit_ref, valid_ref, share_ref, code_ref, stat_ref,
    w_ref, i_ref, j_ref, t_ref, rr_ref, rl_ref, sr_ref, sl_ref,
    cw_ref, ci_ref, cj_ref, ct_ref, crr_ref, crl_ref, csr_ref, csl_ref,
    send_sem, recv_sem, local_sem, fan_sem, right_sem, left_sem, relay_sem, far_sem,
    stat_send, stat_recv, pair_send, pair_recv, chain_send, chain_recv,
):
    shape = plane_shape(groups)
    nz, ny = shape
    parts = ny
    rows_dev, width = points_ref.shape
    kids = cent_ref.shape[0]
    half_kids = kids // 2
    tile = width // LANES
    chunks = width // CHUNK
    block = SEATS * tile
    seat_count = groups * SEATS
    part_rows = 2 * nz * block
    all_rows = cols * seat_count
    score_scale = SHARPNESS / width
    me = lax.axis_index("grp")
    col = lax.axis_index("col")
    core = me % 2
    sibling = me + 1 - 2 * core
    ahead = lax.rem(me + 2, groups)
    behind = lax.rem(me + groups - 2, groups)
    right, left = lax.rem(col + 1, cols), lax.rem(col + cols - 1, cols)
    far = lax.rem(col + 2, cols)

    barrier = pltpu.get_barrier_semaphore()

    def greet(o, carry):
        pl.semaphore_signal(barrier, inc=1, device_id=(peer(me, o, shape), col), device_id_type=MESH)
        return carry

    lax.fori_loop(1, groups, greet, 0)
    for other in (right, left, far):
        pl.semaphore_signal(barrier, inc=1, device_id=(me, other), device_id_type=MESH)

    labels = jnp.broadcast_to(labels_ref[...], (rows_dev, rows_dev))
    r = lax.broadcasted_iota(jnp.int32, (rows_dev, rows_dev), 0)
    c = lax.broadcasted_iota(jnp.int32, (rows_dev, rows_dev), 1)
    before = (labels == labels.T) & (r < c)
    rank = jnp.sum(before.astype(F32), axis=0, keepdims=True)
    mine = labels_ref[...]
    first = jnp.zeros_like(mine)
    for p in range(bounds_ref.shape[0] - 1):
        first = jnp.where(mine == p, bounds_ref[p].astype(F32), first)
    seat = (first * SEATS + rank).astype(jnp.int32)
    s = lax.broadcasted_iota(jnp.int32, (seat_count, rows_dev), 0)
    pick = (s == jnp.broadcast_to(seat, (seat_count, rows_dev))).astype(F32)
    empty = 1.0 - jnp.sum(pick, axis=1, keepdims=True)
    lane = lax.broadcasted_iota(jnp.int32, (seat_count, LANES), 1)
    for q in range(tile):
        part = jnp.dot(pick, points_ref[:, q * LANES : (q + 1) * LANES], precision=HIGHEST)
        if q == 0:
            part = part + jnp.where(lane == 0, empty * MARK, 0.0)
        seats_ref[pl.ds(q, seat_count, stride=tile), :] = part

    pl.semaphore_wait(barrier, groups - 1 + 3)

    def place(k, source, lo, size):
        base = (k * cols + source) * part_rows + lo
        return rows_ref.at[pl.ds(pl.multiple_of(base, 8), size), :]

    def own_copy():
        return pltpu.make_async_copy(
            seats_ref.at[pl.ds(pl.multiple_of(me * block, block), block), :],
            place(0, col, 0, block),
            local_sem,
        )

    def send(o, carry):
        to = peer(me, o, shape)
        k = o // (2 * nz)
        pltpu.make_async_remote_copy(
            src_ref=seats_ref.at[pl.ds(pl.multiple_of(to * block, block), block), :],
            dst_ref=place(k, col, (o % (2 * nz)) * block, block),
            send_sem=send_sem,
            recv_sem=recv_sem.at[k],
            device_id=(to, col),
            device_id_type=MESH,
        ).start()
        return carry

    def link(src, dst, ssem, rsem, to):
        return pltpu.make_async_remote_copy(
            src_ref=src, dst_ref=dst, send_sem=ssem, recv_sem=rsem,
            device_id=to, device_id_type=MESH,
        )

    half = part_rows // 2

    def to_right(k, source):
        cut = place(k, source, 0, part_rows)
        return link(cut, cut, fan_sem.at[0, k], right_sem.at[k], (me, right))

    def to_left(k, source):
        cut = place(k, source, 0, part_rows)
        return link(cut, cut, fan_sem.at[1, k], left_sem.at[k], (me, left))

    def on_right(k, source):
        cut = place(k, source, 0, half)
        return link(cut, cut, relay_sem.at[0, k], far_sem.at[0, k], (me, right))

    def on_left(k, source):
        cut = place(k, source, half, half)
        return link(cut, cut, relay_sem.at[1, k], far_sem.at[1, k], (me, left))

    def arrived(k):
        lo = block if k == 0 else 0
        cut = place(k, col, lo, part_rows - lo)
        link(cut, cut, send_sem, recv_sem.at[k], (me, right)).wait_recv()

    def relay(k):
        to_right(k, left).wait_recv()
        on_right(k, left).start()
        to_left(k, right).wait_recv()
        on_left(k, right).start()

    def settled(k):
        on_right(k, far).wait_recv()
        on_left(k, far).wait_recv()

    def encode(d, block_of_c):
        hi, lo = halves(block_of_c)
        code_ref[d, :kids, :] = hi
        code_ref[d, kids:, :] = lo

    def score(d, lo, size):
        a = dot_nt(code_ref[d], xh_ref[d, lo : lo + size, :])
        b = dot_nt(code_ref[d, :kids, :], xl_ref[d, lo : lo + size, :])
        return a[:kids] + a[kids:] + b

    pick_mark = (
        (lax.broadcasted_iota(jnp.int32, (16, CHUNK), 0) == 0)
        & (lax.broadcasted_iota(jnp.int32, (16, CHUNK), 1) == 0)
    ).astype(BF16)
    batch = 2 * cols * part_rows // tile

    def absorb(b):
        lo = b * batch
        for q in range(tile):
            hi, rest = halves(rows_ref[pl.ds(lo * tile + q, batch, stride=tile), :])
            d, at = q // (CHUNK // LANES), (q % (CHUNK // LANES)) * LANES
            xh_ref[d, lo : lo + batch, at : at + LANES] = hi
            xl_ref[d, lo : lo + batch, at : at + LANES] = rest
        total = score(0, lo, batch)
        for d in range(1, chunks):
            total = total + score(d, lo, batch)
        logit_ref[:, lo : lo + batch] = total
        mark = dot_nt(pick_mark, xh_ref[0, lo : lo + batch, :])[0:1]
        valid_ref[:, lo : lo + batch] = (mark < 0.5 * MARK).astype(F32)

    own_copy().start()
    lax.fori_loop(1, WINDOW * 2 * nz, send, 0)
    own_copy().wait()
    half_norm = jnp.zeros((kids, 1), F32)
    for d in range(chunks):
        now = cent_ref[:, d * CHUNK : (d + 1) * CHUNK]
        encode(d, now)
        half_norm = half_norm + 0.5 * jnp.sum(now * now, axis=1, keepdims=True)

    for k in range(parts):
        arrived(k)
        to_right(k, col).start()
        to_left(k, col).start()
        if k + WINDOW < parts:
            lax.fori_loop((k + WINDOW) * 2 * nz, (k + WINDOW + 1) * 2 * nz, send, 0)
        if k >= 1:
            relay(k - 1)
        if k >= 3 and k % 2 == 1:
            settled(k - 3)
            settled(k - 2)
            absorb((k - 3) // 2)
    relay(parts - 1)
    settled(parts - 2)
    settled(parts - 1)
    absorb(parts // 2 - 1)

    chip = me // 2

    def owner(g):
        count = jnp.zeros((), jnp.int32)
        for p in range(1, bounds_ref.shape[0]):
            count = count + (bounds_ref[p] <= g).astype(jnp.int32)
        return count

    owner0, owner1 = owner(2 * chip), owner(2 * chip + 1)
    same = (owner0 == owner1).astype(F32)
    from_left = ((owner(2 * chip - 1) == owner0) & (chip > 0)).astype(F32)
    from_right = (owner(2 * chip + 2) == owner1).astype(F32)
    through_left, through_right = same * from_left, same * from_right
    is0 = core == 0
    mine_left = jnp.where(is0, from_left, through_left)
    mine_right = jnp.where(is0, through_right, from_right)
    other_left = jnp.where(is0, through_left, from_left)
    other_right = jnp.where(is0, from_right, through_right)
    my_half = pl.multiple_of(core * half_kids, half_kids)
    its_half = pl.multiple_of((1 - core) * half_kids, half_kids)

    for it in range(ITERS):
        peak = jnp.full((1, all_rows), -jnp.inf, F32)
        logits = (logit_ref[...] - half_norm) * score_scale
        peak = jnp.max(logits, axis=0, keepdims=True)
        raised = jnp.exp(logits - peak)
        logit_ref[...] = raised
        stat_ref[it, 0, 0:1, :] = peak
        stat_ref[it, 0, 1:2, :] = jnp.sum(raised, axis=0, keepdims=True)
        stats = [
            link(stat_ref.at[it, 0], stat_ref.at[it, 1 + n], stat_send.at[it, n], stat_recv.at[it, n], (me, to))
            for n, to in enumerate((right, left, far))
        ]
        for copy in stats:
            copy.start()
        for copy in stats:
            copy.wait()
        top = peak
        for n in range(3):
            top = jnp.maximum(top, stat_ref[it, 1 + n, 0:1, :])
        denominator = jnp.zeros((1, all_rows), F32)
        for n in range(4):
            denominator = denominator + stat_ref[it, n, 1:2, :] * jnp.exp(stat_ref[it, n, 0:1, :] - top)
        scale = valid_ref[...] * jnp.exp(peak - top) / denominator
        shares = logit_ref[...] * scale
        hi, lo = halves(shares)
        share_ref[:kids, :] = hi
        share_ref[kids:, :] = lo
        cw_ref[it, 0] = jnp.broadcast_to(jnp.sum(shares, axis=1, keepdims=True), (kids, LANES))

        def bufs(n):
            if n == 0:
                refs = (cw_ref, ci_ref, cj_ref, ct_ref, crr_ref, crl_ref, csr_ref, csl_ref)
                return [ref.at[it, 0] for ref in refs]
            refs = (w_ref, i_ref, j_ref, t_ref, rr_ref, rl_ref, sr_ref, sl_ref)
            return [ref.at[it, n - 1] for ref in refs]

        def swap(n):
            w, i = bufs(n)[:2]
            return link(w.at[pl.ds(its_half, half_kids), :], i, pair_send.at[it, 0, n], pair_recv.at[it, 0, n], (sibling, col))

        def swap_back(n):
            j, t = bufs(n)[2:4]
            return link(t, j, pair_send.at[it, 1, n], pair_recv.at[it, 1, n], (sibling, col))

        def shift_right(n, m):
            b = bufs(n)
            return link(b[6].at[m], b[4].at[m], chain_send.at[it, 0, n, m], chain_recv.at[it, 0, n, m], (ahead, col))

        def shift_left(n, m):
            b = bufs(n)
            return link(b[7].at[m], b[5].at[m], chain_send.at[it, 1, n, m], chain_recv.at[it, 1, n, m], (behind, col))

        def begin(n):
            swap(n).wait_recv()
            b = bufs(n)
            own, its = b[0][pl.ds(my_half, half_kids), :], b[1][...]
            b[7][0] = jnp.where(is0, own + same * its, its + same * own)
            b[6][0] = jnp.where(is0, its + same * own, own + same * its)
            shift_right(n, 0).start()
            shift_left(n, 0).start()

        swap(0).start()
        for d in range(chunks):
            both = dot_nn(share_ref[...], xh_ref[d])
            rest = dot_nn(share_ref[:kids, :], xl_ref[d])
            w_ref[it, d] = both[:kids] + both[kids:] + rest
            swap(d + 1).start()
            begin(d)
        begin(chunks)
        for m in range(ROUNDS - 1):
            for n in range(chunks + 1):
                b = bufs(n)
                shift_right(n, m).wait_recv()
                b[6][m + 1] = b[6][0] + through_left * b[4][m]
                shift_right(n, m + 1).start()
                shift_left(n, m).wait_recv()
                b[7][m + 1] = b[7][0] + through_right * b[5][m]
                shift_left(n, m + 1).start()
        for n in range(chunks + 1):
            b = bufs(n)
            shift_right(n, ROUNDS - 1).wait_recv()
            shift_left(n, ROUNDS - 1).wait_recv()
            from_l, from_r = b[4][ROUNDS - 1], b[5][ROUNDS - 1]
            toward0, toward1 = b[7][0], b[6][0]
            b[3][...] = jnp.where(is0, toward1, toward0) + other_left * from_l + other_right * from_r
            swap_back(n).start()
            b[0][pl.ds(my_half, half_kids), :] = (
                jnp.where(is0, toward0, toward1) + mine_left * from_l + mine_right * from_r
            )
        swap(0).wait_send()
        swap_back(0).wait_recv()
        cw_ref[it, 0, pl.ds(its_half, half_kids), :] = cj_ref[it, 0]
        shrink = 1.0 / (cw_ref[it, 0] + 1.0)
        shrink = jnp.concatenate([shrink] * (CHUNK // LANES), axis=1)
        source = cent_ref if it == 0 else out_ref
        half_norm = jnp.zeros((kids, 1), F32)
        for d in range(chunks):
            swap(d + 1).wait_send()
            swap_back(d + 1).wait_recv()
            w_ref[it, d, pl.ds(its_half, half_kids), :] = j_ref[it, d]
            at = slice(d * CHUNK, (d + 1) * CHUNK)
            now = (w_ref[it, d] + source[:, at]) * shrink
            out_ref[:, at] = now
            if it + 1 < ITERS:
                encode(d, now)
                half_norm = half_norm + 0.5 * jnp.sum(now * now, axis=1, keepdims=True)
                for b in range(all_rows // batch):
                    lo = b * batch
                    scored = score(d, lo, batch)
                    if d > 0:
                        scored = scored + logit_ref[:, lo : lo + batch]
                    logit_ref[:, lo : lo + batch] = scored
        for n in range(chunks + 1):
            swap_back(n).wait_send()
            for m in range(ROUNDS):
                shift_right(n, m).wait_send()
                shift_left(n, m).wait_send()

    for k in range(parts):
        to_right(k, col).wait_send()
        to_left(k, col).wait_send()
        on_right(k, left).wait_send()
        on_left(k, right).wait_send()
    sent = seats_ref.at[pl.ds(0, (groups - 1) * block), :]
    link(sent, sent, send_sem, recv_sem.at[0], (me, right)).wait_send()


def on_device(points, labels, boundaries, centroids):
    groups = lax.axis_size("grp")
    cols = lax.axis_size("col")
    rows, width = points.shape
    kids = centroids.shape[1]
    tile = width // LANES
    parts = plane_shape(groups)[1]
    seat_count = groups * SEATS
    all_rows = cols * seat_count
    chunks = width // CHUNK
    dma = pltpu.SemaphoreType.DMA
    vmem = pl.BlockSpec(memory_space=pltpu.VMEM)

    def sums_scratch(count, lanes):
        half = kids // 2
        one = pltpu.VMEM((ITERS, count, half, lanes), F32)
        many = pltpu.VMEM((ITERS, count, ROUNDS, half, lanes), F32)
        return [pltpu.VMEM((ITERS, count, kids, lanes), F32), one, one, one, many, many, many, many]

    out = pl.pallas_call(
        functools.partial(kernel, groups, cols),
        out_shape=jax.ShapeDtypeStruct((kids, width), F32),
        in_specs=[pl.BlockSpec(memory_space=pltpu.SMEM), vmem, vmem, vmem],
        out_specs=vmem,
        scratch_shapes=[
            pltpu.VMEM((seat_count * tile, LANES), F32),
            pltpu.VMEM((all_rows * tile, LANES), F32),
            pltpu.VMEM((chunks, all_rows, CHUNK), BF16),
            pltpu.VMEM((chunks, all_rows, CHUNK), BF16),
            pltpu.VMEM((kids, all_rows), F32),
            pltpu.VMEM((1, all_rows), F32),
            pltpu.VMEM((2 * kids, all_rows), BF16),
            pltpu.VMEM((chunks, 2 * kids, CHUNK), BF16),
            pltpu.VMEM((ITERS, 4, 2, all_rows), F32),
            *sums_scratch(chunks, CHUNK),
            *sums_scratch(1, LANES),
            dma, dma((parts,)), dma, dma((2, parts)), dma((parts,)), dma((parts,)),
            dma((2, parts)), dma((2, parts)),
            dma((ITERS, 3)), dma((ITERS, 3)),
            dma((ITERS, 2, chunks + 1)), dma((ITERS, 2, chunks + 1)),
            dma((ITERS, 2, chunks + 1, ROUNDS)), dma((ITERS, 2, chunks + 1, ROUNDS)),
        ],
        compiler_params=pltpu.CompilerParams(
            collective_id=0, has_side_effects=True, vmem_limit_bytes=48 << 20
        ),
    )(boundaries, labels.astype(F32).reshape(1, rows), points, centroids[0])
    return out[None]


def solution(mesh):
    placed = (P(("grp", "col"), None), P(("grp", "col")), P(), P("grp", "col", None))
    return jax.shard_map(
        on_device, mesh=mesh, in_specs=placed, out_specs=P("grp", "col", None), check_vma=False
    )
```

```python
import functools

import jax
import jax.numpy as jnp
from jax import lax
from jax.experimental import pallas as pl
from jax.experimental.pallas import tpu as pltpu
from jax.sharding import PartitionSpec as P

ITERS = 2
SHARPNESS = 6.0
HIGHEST = lax.Precision.HIGHEST
MESH = pl.DeviceIdType.MESH
LANES = 128
SEATS = 2
MARK = 4096.0
ROUNDS = 3
WINDOW = 3
CHUNK = 256
F32 = jnp.float32
BF16 = jnp.bfloat16


def plane_side(groups):
    side = 1
    while 2 * side * side < groups:
        side *= 2
    return side


def part_steps(k, side):
    return 2 * side if k == 0 else 2 * (side - 1)


def part_first(k, side):
    return 0 if k == 0 else 2 * side + 2 * (side - 1) * (k - 1)


def peer(me, k, step, side):
    core, y, z = me % 2, (me // 2) % side, me // (2 * side)
    j, dc = step // 2, step % 2
    if k == 0:
        dz, dy = j, 0
    elif k == 1:
        dz, dy = 0, j + 1
    else:
        dz, dy = j + 1, 1 + (j + k - 2) % (side - 1)
    return (((z + dz) % side) * side + (y + dy) % side) * 2 + (core + dc) % 2


def tour_place(me, target, side):
    shift = side.bit_length()
    core, y, z = me % 2, (me // 2) % side, me // (2 * side)
    dc = (target - core) & 1
    dy = (lax.shift_right_logical(target, 1) - y) & (side - 1)
    dz = (lax.shift_right_logical(target, shift) - z) & (side - 1)
    turn = dy - dz + jnp.where(dy < dz, side - 1, 0)
    rest = 2 * side + 2 * (side - 1) * (1 + turn) + 2 * (dz - 1) + dc
    return jnp.where(dy == 0, 2 * dz + dc, jnp.where(dz == 0, 2 * side + 2 * (dy - 1) + dc, rest))


def halves(x):
    hi = x.astype(BF16)
    return hi, (x - hi.astype(F32)).astype(BF16)


def dot_nt(a, b):
    return lax.dot_general(a, b, (((1,), (1,)), ((), ())), preferred_element_type=F32)


def dot_nn(a, b):
    return lax.dot_general(a, b, (((1,), (0,)), ((), ())), preferred_element_type=F32)


def kernel(
    groups, cols, bounds_ref, labels_ref, points_hbm, cent_hbm, out_ref,
    points_ref, cent_ref, seats_ref, rows_ref, xh_ref, xl_ref, logit_ref, valid_ref, share_ref, code_ref, stat_ref,
    w_ref, i_ref, j_ref, t_ref, rr_ref, rl_ref, sr_ref, sl_ref,
    cw_ref, ci_ref, crr_ref, crl_ref, csr_ref, csl_ref,
    send_sem, recv_sem, local_sem, fan_sem, right_sem, left_sem, relay_sem, far_sem,
    met_sem, stat_send, stat_recv, pair_send, pair_recv, chain_send, chain_recv,
):
    side = plane_side(groups)
    parts = side + 1
    rows_dev, width = points_ref.shape
    kids = cent_ref.shape[0]
    half_kids = kids // 2
    tile = width // LANES
    chunks = width // CHUNK
    block = SEATS * tile
    seat_count = groups * SEATS
    all_rows = cols * seat_count
    score_scale = SHARPNESS / width
    me = lax.axis_index("grp")
    col = lax.axis_index("col")
    core = me % 2
    sibling = me + 1 - 2 * core
    ahead = lax.rem(me + 2, groups)
    behind = lax.rem(me + groups - 2, groups)
    right, left = lax.rem(col + 1, cols), lax.rem(col + cols - 1, cols)
    far = lax.rem(col + 2, cols)

    barrier = pltpu.get_barrier_semaphore()
    for k in range(2):
        for step in range(part_steps(k, side)):
            if k or step:
                to = peer(me, k, step, side)
                pl.semaphore_signal(barrier, inc=1, device_id=(to, col), device_id_type=MESH)
    for other in (right, left, far):
        pl.semaphore_signal(barrier, inc=1, device_id=(me, other), device_id_type=MESH)

    points_copy = pltpu.make_async_copy(points_hbm, points_ref, local_sem.at[0])
    cent_copy = pltpu.make_async_copy(cent_hbm, cent_ref, local_sem.at[1])
    points_copy.start()
    cent_copy.start()

    mine = labels_ref[...].astype(F32)
    labels = jnp.broadcast_to(mine, (rows_dev, rows_dev))
    r = lax.broadcasted_iota(jnp.int32, (rows_dev, rows_dev), 0)
    c = lax.broadcasted_iota(jnp.int32, (rows_dev, rows_dev), 1)
    before = (labels == labels.T) & (r < c)
    rank = jnp.sum(before.astype(F32), axis=0, keepdims=True)
    first = jnp.zeros_like(mine)
    for p in range(bounds_ref.shape[0] - 1):
        first = jnp.where(mine == p, bounds_ref[p].astype(F32), first)
    seat = (first * SEATS + rank).astype(jnp.int32)
    seat = SEATS * tour_place(me, lax.shift_right_logical(seat, 1), side) + (seat & 1)
    s = lax.broadcasted_iota(jnp.int32, (seat_count, rows_dev), 0)
    pick = (s == jnp.broadcast_to(seat, (seat_count, rows_dev))).astype(F32)
    empty = 1.0 - jnp.sum(pick, axis=1, keepdims=True)
    lane = lax.broadcasted_iota(jnp.int32, (seat_count, LANES), 1)
    points_copy.wait()
    for q in range(tile):
        part = jnp.dot(pick, points_ref[:, q * LANES : (q + 1) * LANES], precision=HIGHEST)
        if q == 0:
            part = part + jnp.where(lane == 0, empty * MARK, 0.0)
        seats_ref[pl.ds(q, seat_count, stride=tile), :] = part

    pl.semaphore_wait(barrier, 4 * side - 3 + 3)
    for dy in range(side - 1):
        to = peer(me, 1, 2 * dy, side)
        pl.semaphore_signal(met_sem, inc=1, device_id=(to, col), device_id_type=MESH)

    def part_rows(k):
        return part_steps(k, side) * block

    def place(k, source, lo, size):
        base = cols * part_first(k, side) * block + source * part_rows(k) + lo
        return rows_ref.at[pl.ds(pl.multiple_of(base, 8), size), :]

    def seated(k, step):
        return seats_ref.at[pl.ds(pl.multiple_of((part_first(k, side) + step) * block, block), block), :]

    def send_part(k):
        def send(step, carry):
            to = peer(me, k, step, side)
            pltpu.make_async_remote_copy(
                src_ref=seated(k, step),
                dst_ref=place(k, col, step * block, block),
                send_sem=send_sem.at[k],
                recv_sem=recv_sem.at[k],
                device_id=(to, col),
                device_id_type=MESH,
            ).start()
            return carry

        lax.fori_loop(0 if k else 1, part_steps(k, side), send, 0)

    def own_copy():
        return pltpu.make_async_copy(seated(0, 0), place(0, col, 0, block), local_sem.at[2])

    def link(src, dst, ssem, rsem, to):
        return pltpu.make_async_remote_copy(
            src_ref=src, dst_ref=dst, send_sem=ssem, recv_sem=rsem,
            device_id=to, device_id_type=MESH,
        )

    def piece(k, source, n):
        half = part_rows(k) // 2
        return place(k, source, n * half, half)

    def to_right(k, source, n):
        cut = piece(k, source, n)
        return link(cut, cut, fan_sem.at[0, n, k], right_sem.at[n, k], (me, right))

    def to_left(k, source, n):
        cut = piece(k, source, n)
        return link(cut, cut, fan_sem.at[1, n, k], left_sem.at[n, k], (me, left))

    def on_right(k, source):
        cut = piece(k, source, 0)
        return link(cut, cut, relay_sem.at[0, k], far_sem.at[0, k], (me, right))

    def on_left(k, source):
        cut = piece(k, source, 1)
        return link(cut, cut, relay_sem.at[1, k], far_sem.at[1, k], (me, left))

    def arrived(k):
        lo = 0 if k else block
        cut = place(k, col, lo, part_rows(k) - lo)
        link(cut, cut, send_sem.at[k], recv_sem.at[k], (me, right)).wait_recv()

    def fan(k):
        to_right(k, col, 0).start()
        to_left(k, col, 1).start()
        to_right(k, col, 1).start()
        to_left(k, col, 0).start()

    def relay(k):
        to_right(k, left, 0).wait_recv()
        on_right(k, left).start()
        to_left(k, right, 1).wait_recv()
        on_left(k, right).start()

    def settled(k):
        to_right(k, left, 1).wait_recv()
        to_left(k, right, 0).wait_recv()
        on_right(k, far).wait_recv()
        on_left(k, far).wait_recv()

    def encode(d, block_of_c):
        hi, lo = halves(block_of_c)
        code_ref[d, :kids, :] = hi
        code_ref[d, kids:, :] = lo

    def score(d, lo, size):
        a = dot_nt(code_ref[d], xh_ref[d, lo : lo + size, :])
        b = dot_nt(code_ref[d, :kids, :], xl_ref[d, lo : lo + size, :])
        return a[:kids] + a[kids:] + b

    pick_mark = (
        (lax.broadcasted_iota(jnp.int32, (16, CHUNK), 0) == 0)
        & (lax.broadcasted_iota(jnp.int32, (16, CHUNK), 1) == 0)
    ).astype(BF16)
    batch = 2 * rows_dev
    spans = [(b * batch, batch) for b in range(all_rows // batch)]
    early_spans = spans[:-1] + [(spans[-1][0] + n * rows_dev, rows_dev) for n in range(2)]
    last_part = [
        min(k for k in range(parts) if cols * SEATS * part_first(k + 1, side) >= lo + size) for lo, size in early_spans
    ]

    def summarize(it, lo, size, half_norm):
        cut = slice(lo, lo + size)
        logits = (logit_ref[:, cut] - half_norm) * score_scale
        peak = jnp.max(logits, axis=0, keepdims=True)
        raised = jnp.exp(logits - peak)
        logit_ref[:, cut] = raised
        stat_ref[it, 0, 0:1, cut] = peak
        stat_ref[it, 0, 1:2, cut] = jnp.sum(raised, axis=0, keepdims=True)

    def absorb(lo, size):
        for q in range(tile):
            hi, rest = halves(rows_ref[pl.ds(lo * tile + q, size, stride=tile), :])
            d, at = q // (CHUNK // LANES), (q % (CHUNK // LANES)) * LANES
            xh_ref[d, lo : lo + size, at : at + LANES] = hi
            xl_ref[d, lo : lo + size, at : at + LANES] = rest
        total = score(0, lo, size)
        for d in range(1, chunks):
            total = total + score(d, lo, size)
        logit_ref[:, lo : lo + size] = total
        mark = dot_nt(pick_mark, xh_ref[0, lo : lo + size, :])[0:1]
        valid_ref[:, lo : lo + size] = (mark < 0.5 * MARK).astype(F32)
        summarize(0, lo, size, half_norm)

    send_part(0)
    send_part(1)
    own_copy().start()
    cent_copy.wait()
    half_norm = jnp.zeros((kids, 1), F32)
    for d in range(chunks):
        now = cent_ref[:, d * CHUNK : (d + 1) * CHUNK]
        encode(d, now)
        half_norm = half_norm + 0.5 * jnp.sum(now * now, axis=1, keepdims=True)

    pl.semaphore_wait(met_sem, side - 1)
    for k in range(2, 2 + WINDOW):
        send_part(k)
    own_copy().wait()
    for k in range(parts):
        arrived(k)
        fan(k)
        if k >= 1 and k + 1 + WINDOW < parts:
            send_part(k + 1 + WINDOW)
        if k >= 1:
            relay(k - 1)
        if k >= 2:
            settled(k - 2)
        if k - 2 in last_part:
            absorb(*early_spans[last_part.index(k - 2)])
    relay(parts - 1)
    for k in (parts - 2, parts - 1):
        settled(k)
        for span, last in zip(early_spans, last_part):
            if last == k:
                absorb(*span)

    chip = me // 2

    def owner(g):
        count = jnp.zeros((), jnp.int32)
        for p in range(1, bounds_ref.shape[0]):
            count = count + (bounds_ref[p] <= g).astype(jnp.int32)
        return count

    owner0, owner1 = owner(2 * chip), owner(2 * chip + 1)
    same = (owner0 == owner1).astype(F32)
    from_left = ((owner(2 * chip - 1) == owner0) & (chip > 0)).astype(F32)
    from_right = (owner(2 * chip + 2) == owner1).astype(F32)
    through_left, through_right = same * from_left, same * from_right
    is0 = core == 0
    mine_left = jnp.where(is0, from_left, through_left)
    mine_right = jnp.where(is0, through_right, from_right)
    other_left = jnp.where(is0, through_left, from_left)
    other_right = jnp.where(is0, from_right, through_right)
    my_half = pl.multiple_of(core * half_kids, half_kids)
    its_half = pl.multiple_of((1 - core) * half_kids, half_kids)

    for it in range(ITERS):
        stats = [
            link(stat_ref.at[it, 0], stat_ref.at[it, 1 + n], stat_send.at[it, n], stat_recv.at[it, n], (me, to))
            for n, to in enumerate((right, left, far))
        ]
        for copy in stats:
            copy.start()
        for copy in stats:
            copy.wait()
        peak = stat_ref[it, 0, 0:1, :]
        top = peak
        for n in range(3):
            top = jnp.maximum(top, stat_ref[it, 1 + n, 0:1, :])
        denominator = jnp.zeros((1, all_rows), F32)
        for n in range(4):
            denominator = denominator + stat_ref[it, n, 1:2, :] * jnp.exp(stat_ref[it, n, 0:1, :] - top)
        scale = valid_ref[...] * jnp.exp(peak - top) / denominator
        shares = logit_ref[...] * scale
        hi, lo = halves(shares)
        share_ref[:kids, :] = hi
        share_ref[kids:, :] = lo
        counted = dot_nt(jnp.ones((16, all_rows), BF16), share_ref[...])[:8]
        cw_ref[it, 0] = counted[:, :kids] + counted[:, kids:]

        def bufs(n):
            if n == 0:
                refs = (cw_ref, ci_ref, ci_ref, ci_ref, crr_ref, crl_ref, csr_ref, csl_ref)
                return [ref.at[it, 0] for ref in refs]
            refs = (w_ref, i_ref, j_ref, t_ref, rr_ref, rl_ref, sr_ref, sl_ref)
            return [ref.at[it, n - 1] for ref in refs]

        def swap(n):
            w, i = bufs(n)[:2]
            src = w.at[pl.ds(its_half, half_kids), :] if n else w
            return link(src, i, pair_send.at[it, 0, n], pair_recv.at[it, 0, n], (sibling, col))

        def swap_back(n):
            j, t = bufs(n)[2:4]
            return link(t, j, pair_send.at[it, 1, n], pair_recv.at[it, 1, n], (sibling, col))

        def shift_right(n, m):
            b = bufs(n)
            return link(b[6].at[m], b[4].at[m], chain_send.at[it, 0, n, m], chain_recv.at[it, 0, n, m], (ahead, col))

        def shift_left(n, m):
            b = bufs(n)
            return link(b[7].at[m], b[5].at[m], chain_send.at[it, 1, n, m], chain_recv.at[it, 1, n, m], (behind, col))

        def begin(n):
            swap(n).wait_recv()
            b = bufs(n)
            own = b[0][pl.ds(my_half, half_kids), :] if n else b[0][...]
            its = b[1][...]
            b[7][0] = jnp.where(is0, own + same * its, its + same * own)
            b[6][0] = jnp.where(is0, its + same * own, own + same * its)
            shift_right(n, 0).start()
            shift_left(n, 0).start()

        swap(0).start()
        for d in range(chunks):
            both = dot_nn(share_ref[...], xh_ref[d])
            rest = dot_nn(share_ref[:kids, :], xl_ref[d])
            w_ref[it, d] = both[:kids] + both[kids:] + rest
            swap(d + 1).start()
            begin(d)
        begin(chunks)
        for m in range(ROUNDS - 1):
            for n in range(chunks + 1):
                b = bufs(n)
                shift_right(n, m).wait_recv()
                b[6][m + 1] = b[6][0] + through_left * b[4][m]
                shift_right(n, m + 1).start()
                shift_left(n, m).wait_recv()
                b[7][m + 1] = b[7][0] + through_right * b[5][m]
                shift_left(n, m + 1).start()
        for n in range(chunks + 1):
            b = bufs(n)
            shift_right(n, ROUNDS - 1).wait_recv()
            shift_left(n, ROUNDS - 1).wait_recv()
            from_l, from_r = b[4][ROUNDS - 1], b[5][ROUNDS - 1]
            toward0, toward1 = b[7][0], b[6][0]
            if n == 0:
                count = jnp.where(is0, toward0, toward1) + mine_left * from_l + mine_right * from_r
                continue
            b[3][...] = jnp.where(is0, toward1, toward0) + other_left * from_l + other_right * from_r
            swap_back(n).start()
            b[0][pl.ds(my_half, half_kids), :] = (
                jnp.where(is0, toward0, toward1) + mine_left * from_l + mine_right * from_r
            )
        swap(0).wait_send()
        shrink = 1.0 / (jnp.broadcast_to(count[0:1, :], (kids, kids)).T + 1.0)
        shrink = jnp.concatenate([shrink] * (CHUNK // kids), axis=1)
        source = cent_ref if it == 0 else out_ref
        half_norm = jnp.zeros((kids, 1), F32)
        for d in range(chunks):
            swap(d + 1).wait_send()
            swap_back(d + 1).wait_recv()
            w_ref[it, d, pl.ds(its_half, half_kids), :] = j_ref[it, d]
            at = slice(d * CHUNK, (d + 1) * CHUNK)
            now = (w_ref[it, d] + source[:, at]) * shrink
            out_ref[:, at] = now
            if it + 1 < ITERS:
                encode(d, now)
                half_norm = half_norm + 0.5 * jnp.sum(now * now, axis=1, keepdims=True)
                for lo, size in spans:
                    scored = score(d, lo, size)
                    if d > 0:
                        scored = scored + logit_ref[:, lo : lo + size]
                    logit_ref[:, lo : lo + size] = scored
                    if d == chunks - 1:
                        summarize(it + 1, lo, size, half_norm)
        for n in range(chunks + 1):
            if n:
                swap_back(n).wait_send()
            for m in range(ROUNDS):
                shift_right(n, m).wait_send()
                shift_left(n, m).wait_send()

    for k in range(parts):
        for n in range(2):
            to_right(k, col, n).wait_send()
            to_left(k, col, n).wait_send()
        on_right(k, left).wait_send()
        on_left(k, right).wait_send()
        lo = 0 if k else block
        sent = place(k, col, lo, part_rows(k) - lo)
        link(sent, sent, send_sem.at[k], recv_sem.at[k], (me, right)).wait_send()


def on_device(points, labels, boundaries, centroids):
    groups = lax.axis_size("grp")
    cols = lax.axis_size("col")
    rows, width = points.shape
    kids = centroids.shape[1]
    tile = width // LANES
    side = plane_side(groups)
    parts = side + 1
    seat_count = groups * SEATS
    all_rows = cols * seat_count
    chunks = width // CHUNK
    dma = pltpu.SemaphoreType.DMA
    vmem = pl.BlockSpec(memory_space=pltpu.VMEM)
    in_hbm = pl.BlockSpec(memory_space=pl.ANY)

    half = kids // 2
    one = pltpu.VMEM((ITERS, chunks, half, CHUNK), F32)
    many = pltpu.VMEM((ITERS, chunks, ROUNDS, half, CHUNK), F32)
    few = pltpu.VMEM((ITERS, 1, 8, kids), F32)
    few_rounds = pltpu.VMEM((ITERS, 1, ROUNDS, 8, kids), F32)

    out = pl.pallas_call(
        functools.partial(kernel, groups, cols),
        out_shape=jax.ShapeDtypeStruct((kids, width), F32),
        in_specs=[pl.BlockSpec(memory_space=pltpu.SMEM), vmem, in_hbm, in_hbm],
        out_specs=vmem,
        scratch_shapes=[
            pltpu.VMEM((rows, width), F32),
            pltpu.VMEM((kids, width), F32),
            pltpu.VMEM((seat_count * tile, LANES), F32),
            pltpu.VMEM((all_rows * tile, LANES), F32),
            pltpu.VMEM((chunks, all_rows, CHUNK), BF16),
            pltpu.VMEM((chunks, all_rows, CHUNK), BF16),
            pltpu.VMEM((kids, all_rows), F32),
            pltpu.VMEM((1, all_rows), F32),
            pltpu.VMEM((2 * kids, all_rows), BF16),
            pltpu.VMEM((chunks, 2 * kids, CHUNK), BF16),
            pltpu.VMEM((ITERS, 4, 2, all_rows), F32),
            pltpu.VMEM((ITERS, chunks, kids, CHUNK), F32), one, one, one, many, many, many, many,
            few, few, few_rounds, few_rounds, few_rounds, few_rounds,
            dma((parts,)), dma((parts,)), dma((3,)), dma((2, 2, parts)), dma((2, parts)), dma((2, parts)),
            dma((2, parts)), dma((2, parts)),
            pltpu.SemaphoreType.REGULAR,
            dma((ITERS, 3)), dma((ITERS, 3)),
            dma((ITERS, 2, chunks + 1)), dma((ITERS, 2, chunks + 1)),
            dma((ITERS, 2, chunks + 1, ROUNDS)), dma((ITERS, 2, chunks + 1, ROUNDS)),
        ],
        compiler_params=pltpu.CompilerParams(
            collective_id=0, has_side_effects=True, vmem_limit_bytes=56 << 20
        ),
    )(boundaries, labels.reshape(1, rows), points, centroids[0])
    return out[None]


def solution(mesh):
    placed = (P(("grp", "col"), None), P(("grp", "col")), P(), P("grp", "col", None))
    return jax.shard_map(
        on_device, mesh=mesh, in_specs=placed, out_specs=P("grp", "col", None), check_vma=False
    )
```

```python
import functools

import jax
import jax.numpy as jnp
from jax import lax
from jax.experimental import pallas as pl
from jax.experimental.pallas import tpu as pltpu
from jax.sharding import PartitionSpec as P

ITERS = 2
SHARPNESS = 6.0
HIGHEST = lax.Precision.HIGHEST
MESH = pl.DeviceIdType.MESH
LANES = 128
SEATS = 2
MARK = 4096.0
ROUNDS = 3
WINDOW = 4
CHUNK = 256
F32 = jnp.float32
BF16 = jnp.bfloat16


def plane_side(groups):
    side = 1
    while 2 * side * side < groups:
        side *= 2
    return side


def part_steps(k, side):
    return 2 * side if k == 0 else 2 * (side - 1)


def part_first(k, side):
    return 0 if k == 0 else 2 * side + 2 * (side - 1) * (k - 1)


def peer(me, k, step, side):
    core, y, z = me % 2, (me // 2) % side, me // (2 * side)
    j, dc = step // 2, step % 2
    if k == 0:
        dz, dy = j, 0
    elif k == 1:
        dz, dy = 0, j + 1
    else:
        dz, dy = j + 1, 1 + (j + k - 2) % (side - 1)
    return (((z + dz) % side) * side + (y + dy) % side) * 2 + (core + dc) % 2


def tour_place(me, target, side):
    shift = side.bit_length()
    core, y, z = me % 2, (me // 2) % side, me // (2 * side)
    dc = (target - core) & 1
    dy = (lax.shift_right_logical(target, 1) - y) & (side - 1)
    dz = (lax.shift_right_logical(target, shift) - z) & (side - 1)
    turn = dy - dz + jnp.where(dy < dz, side - 1, 0)
    rest = 2 * side + 2 * (side - 1) * (1 + turn) + 2 * (dz - 1) + dc
    return jnp.where(dy == 0, 2 * dz + dc, jnp.where(dz == 0, 2 * side + 2 * (dy - 1) + dc, rest))


def halves(x):
    hi = x.astype(BF16)
    return hi, (x - hi.astype(F32)).astype(BF16)


def dot_nt(a, b):
    return lax.dot_general(a, b, (((1,), (1,)), ((), ())), preferred_element_type=F32)


def dot_nn(a, b):
    return lax.dot_general(a, b, (((1,), (0,)), ((), ())), preferred_element_type=F32)


def kernel(
    groups, cols, bounds_ref, labels_ref, points_hbm, cent_hbm, out_ref,
    points_ref, cent_ref, seats_ref, early_ref, rows_ref, xh_ref, xl_ref, logit_ref, valid_ref, share_ref, code_ref, stat_ref,
    w_ref, i_ref, j_ref, t_ref, rr_ref, rl_ref, sr_ref, sl_ref,
    cw_ref, ci_ref, crr_ref, crl_ref, csr_ref, csl_ref,
    send_sem, recv_sem, local_sem, fan_sem, right_sem, left_sem, relay_sem, far_sem,
    met_sem, stat_send, stat_recv, pair_send, pair_recv, chain_send, chain_recv,
):
    side = plane_side(groups)
    parts = side + 1
    rows_dev, width = points_ref.shape
    kids = cent_ref.shape[0]
    half_kids = kids // 2
    tile = width // LANES
    chunks = width // CHUNK
    block = SEATS * tile
    seat_count = groups * SEATS
    all_rows = cols * seat_count
    score_scale = SHARPNESS / width
    me = lax.axis_index("grp")
    col = lax.axis_index("col")
    core = me % 2
    sibling = me + 1 - 2 * core
    ahead = lax.rem(me + 2, groups)
    behind = lax.rem(me + groups - 2, groups)
    right, left = lax.rem(col + 1, cols), lax.rem(col + cols - 1, cols)
    far = lax.rem(col + 2, cols)

    barrier = pltpu.get_barrier_semaphore()
    for k in range(2):
        for step in range(part_steps(k, side)):
            if k or step:
                to = peer(me, k, step, side)
                pl.semaphore_signal(barrier, inc=1, device_id=(to, col), device_id_type=MESH)
    for other in (right, left, far):
        pl.semaphore_signal(barrier, inc=1, device_id=(me, other), device_id_type=MESH)

    points_copy = pltpu.make_async_copy(points_hbm, points_ref, local_sem.at[0])
    cent_copy = pltpu.make_async_copy(cent_hbm, cent_ref, local_sem.at[1])
    points_copy.start()
    cent_copy.start()

    mine = labels_ref[...].astype(F32)
    labels = jnp.broadcast_to(mine, (rows_dev, rows_dev))
    r = lax.broadcasted_iota(jnp.int32, (rows_dev, rows_dev), 0)
    c = lax.broadcasted_iota(jnp.int32, (rows_dev, rows_dev), 1)
    before = (labels == labels.T) & (r < c)
    rank = jnp.sum(before.astype(F32), axis=0, keepdims=True)
    first = jnp.zeros_like(mine)
    for p in range(bounds_ref.shape[0] - 1):
        first = jnp.where(mine == p, bounds_ref[p].astype(F32), first)
    seat = (first * SEATS + rank).astype(jnp.int32)
    seat = SEATS * tour_place(me, lax.shift_right_logical(seat, 1), side) + (seat & 1)
    s = lax.broadcasted_iota(jnp.int32, (seat_count, rows_dev), 0)
    pick = (s == jnp.broadcast_to(seat, (seat_count, rows_dev))).astype(F32)
    empty = 1.0 - jnp.sum(pick, axis=1, keepdims=True)
    lane = lax.broadcasted_iota(jnp.int32, (seat_count, LANES), 1)
    points_copy.wait()
    for q in range(tile):
        part = jnp.dot(pick, points_ref[:, q * LANES : (q + 1) * LANES], precision=HIGHEST)
        if q == 0:
            part = part + jnp.where(lane == 0, empty * MARK, 0.0)
        seats_ref[pl.ds(q, seat_count, stride=tile), :] = part

    pl.semaphore_wait(barrier, 4 * side - 3 + 3)
    for dy in range(side - 1):
        to = peer(me, 1, 2 * dy, side)
        pl.semaphore_signal(met_sem, inc=1, device_id=(to, col), device_id_type=MESH)

    def part_rows(k):
        return part_steps(k, side) * block

    def place(k, source, lo, size):
        base = cols * part_first(k, side) * block + source * part_rows(k) + lo
        return rows_ref.at[pl.ds(pl.multiple_of(base, 8), size), :]

    last = parts - 1

    def seated(k, step):
        return seats_ref.at[pl.ds(pl.multiple_of((part_first(k, side) + step) * block, block), block), :]

    def send_part(k):
        def send(step, carry):
            to = peer(me, k, step, side)
            pltpu.make_async_remote_copy(
                src_ref=seated(k, step),
                dst_ref=place(k, col, step * block, block),
                send_sem=send_sem.at[k],
                recv_sem=recv_sem.at[k],
                device_id=(to, col),
                device_id_type=MESH,
            ).start()
            return carry

        lax.fori_loop(0 if k else 1, part_steps(k, side), send, 0)

    def send_gathered(source):
        def send(step, carry):
            to = peer(me, last, step, side)
            link(
                early_ref.at[source, pl.ds(pl.multiple_of(step * block, block), block), :],
                place(last, source, step * block, block),
                send_sem.at[last], recv_sem.at[last], (to, col),
            ).start()
            return carry

        lax.fori_loop(0, part_steps(last, side), send, 0)

    def own_copy():
        return pltpu.make_async_copy(seated(0, 0), place(0, col, 0, block), local_sem.at[2])

    def link(src, dst, ssem, rsem, to):
        return pltpu.make_async_remote_copy(
            src_ref=src, dst_ref=dst, send_sem=ssem, recv_sem=rsem,
            device_id=to, device_id_type=MESH,
        )

    def piece(k, source, n):
        half = part_rows(k) // 2
        if k == last:
            return early_ref.at[source, pl.ds(n * half, half), :]
        return place(k, source, n * half, half)

    def start_piece(k, source, n):
        half = part_rows(k) // 2
        if k == last:
            return seats_ref.at[pl.ds(part_first(k, side) * block + n * half, half), :]
        return piece(k, source, n)

    def to_right(k, source, n):
        return link(start_piece(k, source, n), piece(k, source, n), fan_sem.at[0, n, k], right_sem.at[n, k], (me, right))

    def to_left(k, source, n):
        return link(start_piece(k, source, n), piece(k, source, n), fan_sem.at[1, n, k], left_sem.at[n, k], (me, left))

    def on_right(k, source):
        cut = piece(k, source, 0)
        return link(cut, cut, relay_sem.at[0, k], far_sem.at[0, k], (me, right))

    def on_left(k, source):
        cut = piece(k, source, 1)
        return link(cut, cut, relay_sem.at[1, k], far_sem.at[1, k], (me, left))

    def moved(k):
        if k == last:
            return rows_ref.at[pl.ds(cols * part_first(k, side) * block, cols * part_rows(k)), :]
        lo = 0 if k else block
        return place(k, col, lo, part_rows(k) - lo)

    def arrived(k):
        cut = moved(k)
        link(cut, cut, send_sem.at[k], recv_sem.at[k], (me, right)).wait_recv()

    def fan(k):
        to_right(k, col, 0).start()
        to_left(k, col, 1).start()
        to_right(k, col, 1).start()
        to_left(k, col, 0).start()

    def relay(k):
        to_right(k, left, 0).wait_recv()
        on_right(k, left).start()
        to_left(k, right, 1).wait_recv()
        on_left(k, right).start()

    def settled(k):
        to_right(k, left, 1).wait_recv()
        to_left(k, right, 0).wait_recv()
        on_right(k, far).wait_recv()
        on_left(k, far).wait_recv()

    def encode(d, block_of_c):
        hi, lo = halves(block_of_c)
        code_ref[d, :kids, :] = hi
        code_ref[d, kids:, :] = lo

    def score(d, lo, size):
        a = dot_nt(code_ref[d], xh_ref[d, lo : lo + size, :])
        b = dot_nt(code_ref[d, :kids, :], xl_ref[d, lo : lo + size, :])
        return a[:kids] + a[kids:] + b

    pick_mark = (
        (lax.broadcasted_iota(jnp.int32, (16, CHUNK), 0) == 0)
        & (lax.broadcasted_iota(jnp.int32, (16, CHUNK), 1) == 0)
    ).astype(BF16)
    batch = 2 * rows_dev
    spans = [(b * batch, batch) for b in range(all_rows // batch)]
    early_spans = spans[:-1] + [(spans[-1][0] + n * rows_dev, rows_dev) for n in range(2)]
    last_part = [
        min(k for k in range(parts) if cols * SEATS * part_first(k + 1, side) >= lo + size) for lo, size in early_spans
    ]

    def summarize(it, lo, size, half_norm):
        cut = slice(lo, lo + size)
        logits = (logit_ref[:, cut] - half_norm) * score_scale
        peak = jnp.max(logits, axis=0, keepdims=True)
        raised = jnp.exp(logits - peak)
        logit_ref[:, cut] = raised
        stat_ref[it, 0, 0:1, cut] = peak
        stat_ref[it, 0, 1:2, cut] = jnp.sum(raised, axis=0, keepdims=True)

    def absorb(lo, size):
        for q in range(tile):
            hi, rest = halves(rows_ref[pl.ds(lo * tile + q, size, stride=tile), :])
            d, at = q // (CHUNK // LANES), (q % (CHUNK // LANES)) * LANES
            xh_ref[d, lo : lo + size, at : at + LANES] = hi
            xl_ref[d, lo : lo + size, at : at + LANES] = rest
        total = score(0, lo, size)
        for d in range(1, chunks):
            total = total + score(d, lo, size)
        logit_ref[:, lo : lo + size] = total
        mark = dot_nt(pick_mark, xh_ref[0, lo : lo + size, :])[0:1]
        valid_ref[:, lo : lo + size] = (mark < 0.5 * MARK).astype(F32)
        summarize(0, lo, size, half_norm)

    fan(last)
    send_part(0)
    send_part(1)
    own_copy().start()
    cent_copy.wait()
    half_norm = jnp.zeros((kids, 1), F32)
    for d in range(chunks):
        now = cent_ref[:, d * CHUNK : (d + 1) * CHUNK]
        encode(d, now)
        half_norm = half_norm + 0.5 * jnp.sum(now * now, axis=1, keepdims=True)

    pl.semaphore_wait(met_sem, side - 1)
    for k in range(2, 2 + WINDOW):
        send_part(k)
    own_copy().wait()
    relay(last)
    for k in range(last):
        arrived(k)
        fan(k)
        if k == 1:
            for later in range(2 + WINDOW, last):
                send_part(later)
            settled(last)
        if k == 2:
            send_part(last)
        if k == 3:
            send_gathered(left)
        if k == 4:
            send_gathered(right)
        if k == 5:
            send_gathered(far)
        if k >= 1:
            relay(k - 1)
        if k >= 2:
            settled(k - 2)
        if k - 2 in last_part:
            absorb(*early_spans[last_part.index(k - 2)])
    relay(last - 1)
    settled(last - 2)
    for span, need in zip(early_spans, last_part):
        if need == last - 2:
            absorb(*span)
    settled(last - 1)
    arrived(last)
    for span, need in zip(early_spans, last_part):
        if need > last - 2:
            absorb(*span)

    chip = me // 2

    def owner(g):
        count = jnp.zeros((), jnp.int32)
        for p in range(1, bounds_ref.shape[0]):
            count = count + (bounds_ref[p] <= g).astype(jnp.int32)
        return count

    owner0, owner1 = owner(2 * chip), owner(2 * chip + 1)
    same = (owner0 == owner1).astype(F32)
    from_left = ((owner(2 * chip - 1) == owner0) & (chip > 0)).astype(F32)
    from_right = (owner(2 * chip + 2) == owner1).astype(F32)
    through_left, through_right = same * from_left, same * from_right
    is0 = core == 0
    mine_left = jnp.where(is0, from_left, through_left)
    mine_right = jnp.where(is0, through_right, from_right)
    other_left = jnp.where(is0, through_left, from_left)
    other_right = jnp.where(is0, from_right, through_right)
    my_half = pl.multiple_of(core * half_kids, half_kids)
    its_half = pl.multiple_of((1 - core) * half_kids, half_kids)

    for it in range(ITERS):
        stats = [
            link(stat_ref.at[it, 0], stat_ref.at[it, 1 + n], stat_send.at[it, n], stat_recv.at[it, n], (me, to))
            for n, to in enumerate((right, left, far))
        ]
        for copy in stats:
            copy.start()
        for copy in stats:
            copy.wait()
        peak = stat_ref[it, 0, 0:1, :]
        top = peak
        for n in range(3):
            top = jnp.maximum(top, stat_ref[it, 1 + n, 0:1, :])
        denominator = jnp.zeros((1, all_rows), F32)
        for n in range(4):
            denominator = denominator + stat_ref[it, n, 1:2, :] * jnp.exp(stat_ref[it, n, 0:1, :] - top)
        scale = valid_ref[...] * jnp.exp(peak - top) / denominator
        shares = logit_ref[...] * scale
        hi, lo = halves(shares)
        share_ref[:kids, :] = hi
        share_ref[kids:, :] = lo
        counted = dot_nt(jnp.ones((16, all_rows), BF16), share_ref[...])[:8]
        cw_ref[it, 0] = counted[:, :kids] + counted[:, kids:]

        def bufs(n):
            if n == 0:
                refs = (cw_ref, ci_ref, ci_ref, ci_ref, crr_ref, crl_ref, csr_ref, csl_ref)
                return [ref.at[it, 0] for ref in refs]
            refs = (w_ref, i_ref, j_ref, t_ref, rr_ref, rl_ref, sr_ref, sl_ref)
            return [ref.at[it, n - 1] for ref in refs]

        def swap(n):
            w, i = bufs(n)[:2]
            src = w.at[pl.ds(its_half, half_kids), :] if n else w
            return link(src, i, pair_send.at[it, 0, n], pair_recv.at[it, 0, n], (sibling, col))

        def swap_back(n):
            j, t = bufs(n)[2:4]
            return link(t, j, pair_send.at[it, 1, n], pair_recv.at[it, 1, n], (sibling, col))

        def shift_right(n, m):
            b = bufs(n)
            return link(b[6].at[m], b[4].at[m], chain_send.at[it, 0, n, m], chain_recv.at[it, 0, n, m], (ahead, col))

        def shift_left(n, m):
            b = bufs(n)
            return link(b[7].at[m], b[5].at[m], chain_send.at[it, 1, n, m], chain_recv.at[it, 1, n, m], (behind, col))

        def begin(n):
            swap(n).wait_recv()
            b = bufs(n)
            own = b[0][pl.ds(my_half, half_kids), :] if n else b[0][...]
            its = b[1][...]
            b[7][0] = jnp.where(is0, own + same * its, its + same * own)
            b[6][0] = jnp.where(is0, its + same * own, own + same * its)
            shift_right(n, 0).start()
            shift_left(n, 0).start()

        swap(0).start()
        for d in range(chunks):
            both = dot_nn(share_ref[...], xh_ref[d])
            rest = dot_nn(share_ref[:kids, :], xl_ref[d])
            w_ref[it, d] = both[:kids] + both[kids:] + rest
            swap(d + 1).start()
            begin(d)
        begin(chunks)
        for m in range(ROUNDS - 1):
            for n in range(chunks + 1):
                b = bufs(n)
                shift_right(n, m).wait_recv()
                b[6][m + 1] = b[6][0] + through_left * b[4][m]
                shift_right(n, m + 1).start()
                shift_left(n, m).wait_recv()
                b[7][m + 1] = b[7][0] + through_right * b[5][m]
                shift_left(n, m + 1).start()
        for n in range(chunks + 1):
            b = bufs(n)
            shift_right(n, ROUNDS - 1).wait_recv()
            shift_left(n, ROUNDS - 1).wait_recv()
            from_l, from_r = b[4][ROUNDS - 1], b[5][ROUNDS - 1]
            toward0, toward1 = b[7][0], b[6][0]
            if n == 0:
                count = jnp.where(is0, toward0, toward1) + mine_left * from_l + mine_right * from_r
                continue
            b[3][...] = jnp.where(is0, toward1, toward0) + other_left * from_l + other_right * from_r
            swap_back(n).start()
            b[0][pl.ds(my_half, half_kids), :] = (
                jnp.where(is0, toward0, toward1) + mine_left * from_l + mine_right * from_r
            )
        swap(0).wait_send()
        shrink = 1.0 / (jnp.broadcast_to(count[0:1, :], (kids, kids)).T + 1.0)
        shrink = jnp.concatenate([shrink] * (CHUNK // kids), axis=1)
        source = cent_ref if it == 0 else out_ref
        half_norm = jnp.zeros((kids, 1), F32)
        for d in range(chunks):
            swap(d + 1).wait_send()
            swap_back(d + 1).wait_recv()
            w_ref[it, d, pl.ds(its_half, half_kids), :] = j_ref[it, d]
            at = slice(d * CHUNK, (d + 1) * CHUNK)
            now = (w_ref[it, d] + source[:, at]) * shrink
            out_ref[:, at] = now
            if it + 1 < ITERS:
                encode(d, now)
                half_norm = half_norm + 0.5 * jnp.sum(now * now, axis=1, keepdims=True)
                for lo, size in spans:
                    scored = score(d, lo, size)
                    if d > 0:
                        scored = scored + logit_ref[:, lo : lo + size]
                    logit_ref[:, lo : lo + size] = scored
                    if d == chunks - 1:
                        summarize(it + 1, lo, size, half_norm)
        for n in range(chunks + 1):
            if n:
                swap_back(n).wait_send()
            for m in range(ROUNDS):
                shift_right(n, m).wait_send()
                shift_left(n, m).wait_send()

    for k in range(parts):
        for n in range(2):
            to_right(k, col, n).wait_send()
            to_left(k, col, n).wait_send()
        on_right(k, left).wait_send()
        on_left(k, right).wait_send()
        sent = moved(k)
        link(sent, sent, send_sem.at[k], recv_sem.at[k], (me, right)).wait_send()


def on_device(points, labels, boundaries, centroids):
    groups = lax.axis_size("grp")
    cols = lax.axis_size("col")
    rows, width = points.shape
    kids = centroids.shape[1]
    tile = width // LANES
    side = plane_side(groups)
    parts = side + 1
    seat_count = groups * SEATS
    all_rows = cols * seat_count
    chunks = width // CHUNK
    dma = pltpu.SemaphoreType.DMA
    vmem = pl.BlockSpec(memory_space=pltpu.VMEM)
    in_hbm = pl.BlockSpec(memory_space=pl.ANY)

    half = kids // 2
    one = pltpu.VMEM((ITERS, chunks, half, CHUNK), F32)
    many = pltpu.VMEM((ITERS, chunks, ROUNDS, half, CHUNK), F32)
    few = pltpu.VMEM((ITERS, 1, 8, kids), F32)
    few_rounds = pltpu.VMEM((ITERS, 1, ROUNDS, 8, kids), F32)

    out = pl.pallas_call(
        functools.partial(kernel, groups, cols),
        out_shape=jax.ShapeDtypeStruct((kids, width), F32),
        in_specs=[pl.BlockSpec(memory_space=pltpu.SMEM), vmem, in_hbm, in_hbm],
        out_specs=vmem,
        scratch_shapes=[
            pltpu.VMEM((rows, width), F32),
            pltpu.VMEM((kids, width), F32),
            pltpu.VMEM((seat_count * tile, LANES), F32),
            pltpu.VMEM((cols, part_steps(parts - 1, side) * SEATS * tile, LANES), F32),
            pltpu.VMEM((all_rows * tile, LANES), F32),
            pltpu.VMEM((chunks, all_rows, CHUNK), BF16),
            pltpu.VMEM((chunks, all_rows, CHUNK), BF16),
            pltpu.VMEM((kids, all_rows), F32),
            pltpu.VMEM((1, all_rows), F32),
            pltpu.VMEM((2 * kids, all_rows), BF16),
            pltpu.VMEM((chunks, 2 * kids, CHUNK), BF16),
            pltpu.VMEM((ITERS, 4, 2, all_rows), F32),
            pltpu.VMEM((ITERS, chunks, kids, CHUNK), F32), one, one, one, many, many, many, many,
            few, few, few_rounds, few_rounds, few_rounds, few_rounds,
            dma((parts,)), dma((parts,)), dma((3,)), dma((2, 2, parts)), dma((2, parts)), dma((2, parts)),
            dma((2, parts)), dma((2, parts)),
            pltpu.SemaphoreType.REGULAR,
            dma((ITERS, 3)), dma((ITERS, 3)),
            dma((ITERS, 2, chunks + 1)), dma((ITERS, 2, chunks + 1)),
            dma((ITERS, 2, chunks + 1, ROUNDS)), dma((ITERS, 2, chunks + 1, ROUNDS)),
        ],
        compiler_params=pltpu.CompilerParams(
            collective_id=0, has_side_effects=True, vmem_limit_bytes=56 << 20
        ),
    )(boundaries, labels.reshape(1, rows), points, centroids[0])
    return out[None]


def solution(mesh):
    placed = (P(("grp", "col"), None), P(("grp", "col")), P(), P("grp", "col", None))
    return jax.shard_map(
        on_device, mesh=mesh, in_specs=placed, out_specs=P("grp", "col", None), check_vma=False
    )
```

```python
import functools

import jax
import jax.numpy as jnp
from jax import lax
from jax.experimental import pallas as pl
from jax.experimental.pallas import tpu as pltpu
from jax.sharding import PartitionSpec as P

ITERS = 2
SHARPNESS = 6.0
HIGHEST = lax.Precision.HIGHEST
MESH = pl.DeviceIdType.MESH
LANES = 128
SEATS = 2
MARK = 4096.0
ROUNDS = 3
WINDOW = 4
CHUNK = 256
F32 = jnp.float32
BF16 = jnp.bfloat16


def plane_side(groups):
    side = 1
    while 2 * side * side < groups:
        side *= 2
    return side


def part_steps(k, side):
    return 2 * side if k == 0 else 2 * (side - 1)


def part_first(k, side):
    return 0 if k == 0 else 2 * side + 2 * (side - 1) * (k - 1)


def peer(me, k, step, side):
    core, y, z = me % 2, (me // 2) % side, me // (2 * side)
    j, dc = step // 2, step % 2
    if k == 0:
        dz, dy = j, 0
    elif k == 1:
        dz, dy = 0, j + 1
    else:
        dz, dy = j + 1, 1 + (j + k - 2) % (side - 1)
    return (((z + dz) % side) * side + (y + dy) % side) * 2 + (core + dc) % 2


def tour_place(me, target, side):
    shift = side.bit_length()
    core, y, z = me % 2, (me // 2) % side, me // (2 * side)
    dc = (target - core) & 1
    dy = (lax.shift_right_logical(target, 1) - y) & (side - 1)
    dz = (lax.shift_right_logical(target, shift) - z) & (side - 1)
    turn = dy - dz + jnp.where(dy < dz, side - 1, 0)
    rest = 2 * side + 2 * (side - 1) * (1 + turn) + 2 * (dz - 1) + dc
    return jnp.where(dy == 0, 2 * dz + dc, jnp.where(dz == 0, 2 * side + 2 * (dy - 1) + dc, rest))


def halves(x):
    hi = x.astype(BF16)
    return hi, (x - hi.astype(F32)).astype(BF16)


def dot_nt(a, b):
    return lax.dot_general(a, b, (((1,), (1,)), ((), ())), preferred_element_type=F32)


def dot_nn(a, b):
    return lax.dot_general(a, b, (((1,), (0,)), ((), ())), preferred_element_type=F32)


def kernel(
    groups, cols, bounds_ref, labels_ref, points_hbm, cent_hbm, out_ref,
    points_ref, cent_ref, seats_ref, early_ref, rows_ref, xh_ref, xl_ref, logit_ref, valid_ref, share_ref, code_ref, stat_ref,
    w_ref, i_ref, j_ref, t_ref, rr_ref, rl_ref, sr_ref, sl_ref,
    cw_ref, ci_ref, crr_ref, crl_ref, csr_ref, csl_ref,
    send_sem, recv_sem, local_sem, fan_sem, right_sem, left_sem, relay_sem, far_sem,
    met_sem, stat_send, stat_recv, pair_send, pair_recv, chain_send, chain_recv,
):
    side = plane_side(groups)
    parts = side + 1
    rows_dev, width = points_ref.shape
    kids = cent_ref.shape[0]
    half_kids = kids // 2
    tile = width // LANES
    chunks = width // CHUNK
    block = SEATS * tile
    seat_count = groups * SEATS
    all_rows = cols * seat_count
    score_scale = SHARPNESS / width
    me = lax.axis_index("grp")
    col = lax.axis_index("col")
    core = me % 2
    sibling = me + 1 - 2 * core
    ahead = lax.rem(me + 2, groups)
    behind = lax.rem(me + groups - 2, groups)
    right, left = lax.rem(col + 1, cols), lax.rem(col + cols - 1, cols)
    far = lax.rem(col + 2, cols)

    barrier = pltpu.get_barrier_semaphore()
    for k in range(2):
        for step in range(part_steps(k, side)):
            if k or step:
                to = peer(me, k, step, side)
                pl.semaphore_signal(barrier, inc=1, device_id=(to, col), device_id_type=MESH)
    for other in (right, left, far):
        pl.semaphore_signal(barrier, inc=1, device_id=(me, other), device_id_type=MESH)

    points_copy = pltpu.make_async_copy(points_hbm, points_ref, local_sem.at[0])
    cent_copy = pltpu.make_async_copy(cent_hbm, cent_ref, local_sem.at[1])
    points_copy.start()
    cent_copy.start()

    mine = labels_ref[...].astype(F32)
    labels = jnp.broadcast_to(mine, (rows_dev, rows_dev))
    r = lax.broadcasted_iota(jnp.int32, (rows_dev, rows_dev), 0)
    c = lax.broadcasted_iota(jnp.int32, (rows_dev, rows_dev), 1)
    before = (labels == labels.T) & (r < c)
    rank = jnp.sum(before.astype(F32), axis=0, keepdims=True)
    first = jnp.zeros_like(mine)
    for p in range(bounds_ref.shape[0] - 1):
        first = jnp.where(mine == p, bounds_ref[p].astype(F32), first)
    seat = (first * SEATS + rank).astype(jnp.int32)
    seat = SEATS * tour_place(me, lax.shift_right_logical(seat, 1), side) + (seat & 1)
    s = lax.broadcasted_iota(jnp.int32, (seat_count, rows_dev), 0)
    pick = (s == jnp.broadcast_to(seat, (seat_count, rows_dev))).astype(F32)
    empty = 1.0 - jnp.sum(pick, axis=1, keepdims=True)
    lane = lax.broadcasted_iota(jnp.int32, (seat_count, LANES), 1)
    points_copy.wait()
    for q in range(tile):
        part = jnp.dot(pick, points_ref[:, q * LANES : (q + 1) * LANES], precision=HIGHEST)
        if q == 0:
            part = part + jnp.where(lane == 0, empty * MARK, 0.0)
        seats_ref[pl.ds(q, seat_count, stride=tile), :] = part

    pl.semaphore_wait(barrier, 4 * side - 3 + 3)
    for dy in range(side - 1):
        to = peer(me, 1, 2 * dy, side)
        pl.semaphore_signal(met_sem, inc=1, device_id=(to, col), device_id_type=MESH)

    def part_rows(k):
        return part_steps(k, side) * block

    def place(k, source, lo, size):
        base = cols * part_first(k, side) * block + source * part_rows(k) + lo
        return rows_ref.at[pl.ds(pl.multiple_of(base, 8), size), :]

    last = parts - 1

    def seated(k, step):
        return seats_ref.at[pl.ds(pl.multiple_of((part_first(k, side) + step) * block, block), block), :]

    def send_part(k):
        def send(step, carry):
            to = peer(me, k, step, side)
            pltpu.make_async_remote_copy(
                src_ref=seated(k, step),
                dst_ref=place(k, col, step * block, block),
                send_sem=send_sem.at[k],
                recv_sem=recv_sem.at[k],
                device_id=(to, col),
                device_id_type=MESH,
            ).start()
            return carry

        lax.fori_loop(0 if k else 1, part_steps(k, side), send, 0)

    def send_gathered(source):
        def send(step, carry):
            to = peer(me, last, step, side)
            link(
                early_ref.at[source, pl.ds(pl.multiple_of(step * block, block), block), :],
                place(last, source, step * block, block),
                send_sem.at[last], recv_sem.at[last], (to, col),
            ).start()
            return carry

        lax.fori_loop(0, part_steps(last, side), send, 0)

    def own_copy():
        return pltpu.make_async_copy(seated(0, 0), place(0, col, 0, block), local_sem.at[2])

    def link(src, dst, ssem, rsem, to):
        return pltpu.make_async_remote_copy(
            src_ref=src, dst_ref=dst, send_sem=ssem, recv_sem=rsem,
            device_id=to, device_id_type=MESH,
        )

    def piece(k, source, n):
        half = part_rows(k) // 2
        if k == last:
            return early_ref.at[source, pl.ds(n * half, half), :]
        return place(k, source, n * half, half)

    def start_piece(k, source, n):
        half = part_rows(k) // 2
        if k == last:
            return seats_ref.at[pl.ds(part_first(k, side) * block + n * half, half), :]
        return piece(k, source, n)

    def to_right(k, source, n):
        return link(start_piece(k, source, n), piece(k, source, n), fan_sem.at[0, n, k], right_sem.at[n, k], (me, right))

    def to_left(k, source, n):
        return link(start_piece(k, source, n), piece(k, source, n), fan_sem.at[1, n, k], left_sem.at[n, k], (me, left))

    def on_right(k, source):
        cut = piece(k, source, 0)
        return link(cut, cut, relay_sem.at[0, k], far_sem.at[0, k], (me, right))

    def on_left(k, source):
        cut = piece(k, source, 1)
        return link(cut, cut, relay_sem.at[1, k], far_sem.at[1, k], (me, left))

    def moved(k):
        if k == last:
            return rows_ref.at[pl.ds(cols * part_first(k, side) * block, cols * part_rows(k)), :]
        lo = 0 if k else block
        return place(k, col, lo, part_rows(k) - lo)

    def arrived(k):
        cut = moved(k)
        link(cut, cut, send_sem.at[k], recv_sem.at[k], (me, right)).wait_recv()

    def fan(k):
        to_right(k, col, 0).start()
        to_left(k, col, 1).start()
        to_right(k, col, 1).start()
        to_left(k, col, 0).start()

    def relay(k):
        to_right(k, left, 0).wait_recv()
        on_right(k, left).start()
        to_left(k, right, 1).wait_recv()
        on_left(k, right).start()

    def settled(k):
        to_right(k, left, 1).wait_recv()
        to_left(k, right, 0).wait_recv()
        on_right(k, far).wait_recv()
        on_left(k, far).wait_recv()

    def encode(d, block_of_c):
        hi, lo = halves(block_of_c)
        code_ref[d, :kids, :] = hi
        code_ref[d, kids:, :] = lo

    def score(d, lo, size):
        a = dot_nt(code_ref[d], xh_ref[d, lo : lo + size, :])
        b = dot_nt(code_ref[d, :kids, :], xl_ref[d, lo : lo + size, :])
        return a[:kids] + a[kids:] + b

    pick_mark = (
        (lax.broadcasted_iota(jnp.int32, (16, CHUNK), 0) == 0)
        & (lax.broadcasted_iota(jnp.int32, (16, CHUNK), 1) == 0)
    ).astype(BF16)
    batch = 2 * rows_dev
    spans = [(b * batch, batch) for b in range(all_rows // batch)]
    early_spans = spans[:-1] + [(spans[-1][0] + n * rows_dev, rows_dev) for n in range(2)]
    last_part = [
        min(k for k in range(parts) if cols * SEATS * part_first(k + 1, side) >= lo + size) for lo, size in early_spans
    ]

    def summarize(it, lo, size, half_norm):
        cut = slice(lo, lo + size)
        logits = (logit_ref[:, cut] - half_norm) * score_scale
        peak = jnp.max(logits, axis=0, keepdims=True)
        raised = jnp.exp(logits - peak)
        logit_ref[:, cut] = raised
        stat_ref[it, 0, 0:1, cut] = peak
        stat_ref[it, 0, 1:2, cut] = jnp.sum(raised, axis=0, keepdims=True)

    def absorb(lo, size):
        for q in range(tile):
            hi, rest = halves(rows_ref[pl.ds(lo * tile + q, size, stride=tile), :])
            d, at = q // (CHUNK // LANES), (q % (CHUNK // LANES)) * LANES
            xh_ref[d, lo : lo + size, at : at + LANES] = hi
            xl_ref[d, lo : lo + size, at : at + LANES] = rest
        total = score(0, lo, size)
        for d in range(1, chunks):
            total = total + score(d, lo, size)
        logit_ref[:, lo : lo + size] = total
        mark = dot_nt(pick_mark, xh_ref[0, lo : lo + size, :])[0:1]
        valid_ref[:, lo : lo + size] = (mark < 0.5 * MARK).astype(F32)
        summarize(0, lo, size, half_norm)

    fan(last)
    send_part(0)
    send_part(1)
    own_copy().start()
    cent_copy.wait()
    half_norm = jnp.zeros((kids, 1), F32)
    for d in range(chunks):
        now = cent_ref[:, d * CHUNK : (d + 1) * CHUNK]
        encode(d, now)
        half_norm = half_norm + 0.5 * jnp.sum(now * now, axis=1, keepdims=True)

    pl.semaphore_wait(met_sem, side - 1)
    for k in range(2, 2 + WINDOW):
        send_part(k)
    own_copy().wait()
    relay(last)
    for k in range(last):
        arrived(k)
        fan(k)
        if k == 1:
            for later in range(2 + WINDOW, last):
                send_part(later)
            settled(last)
        if k == 2:
            send_part(last)
        if k == 3:
            send_gathered(left)
        if k == 4:
            send_gathered(right)
        if k == 5:
            send_gathered(far)
        if k >= 1:
            relay(k - 1)
        if k >= 2:
            settled(k - 2)
        if k - 2 in last_part:
            absorb(*early_spans[last_part.index(k - 2)])
    relay(last - 1)
    settled(last - 2)
    for span, need in zip(early_spans, last_part):
        if need == last - 2:
            absorb(*span)
    settled(last - 1)
    arrived(last)
    for span, need in zip(early_spans, last_part):
        if need > last - 2:
            absorb(*span)

    chip = me // 2

    def owner(g):
        count = jnp.zeros((), jnp.int32)
        for p in range(1, bounds_ref.shape[0]):
            count = count + (bounds_ref[p] <= g).astype(jnp.int32)
        return count

    owner0, owner1 = owner(2 * chip), owner(2 * chip + 1)
    same = (owner0 == owner1).astype(F32)
    from_left = ((owner(2 * chip - 1) == owner0) & (chip > 0)).astype(F32)
    from_right = (owner(2 * chip + 2) == owner1).astype(F32)
    through_left, through_right = same * from_left, same * from_right
    is0 = core == 0
    mine_left = jnp.where(is0, from_left, through_left)
    mine_right = jnp.where(is0, through_right, from_right)
    other_left = jnp.where(is0, through_left, from_left)
    other_right = jnp.where(is0, from_right, through_right)
    my_half = pl.multiple_of(core * half_kids, half_kids)
    its_half = pl.multiple_of((1 - core) * half_kids, half_kids)

    for it in range(ITERS):
        stats = [
            link(stat_ref.at[it, 0], stat_ref.at[it, 1 + n], stat_send.at[it, n], stat_recv.at[it, n], (me, to))
            for n, to in enumerate((right, left, far))
        ]
        for copy in stats:
            copy.start()
        for copy in stats:
            copy.wait()
        peak = stat_ref[it, 0, 0:1, :]
        top = peak
        for n in range(3):
            top = jnp.maximum(top, stat_ref[it, 1 + n, 0:1, :])
        denominator = jnp.zeros((1, all_rows), F32)
        for n in range(4):
            denominator = denominator + stat_ref[it, n, 1:2, :] * jnp.exp(stat_ref[it, n, 0:1, :] - top)
        scale = valid_ref[...] * jnp.exp(peak - top) / denominator
        shares = logit_ref[...] * scale
        hi, lo = halves(shares)
        share_ref[:kids, :] = hi
        share_ref[kids:, :] = lo
        counted = dot_nt(jnp.ones((16, all_rows), BF16), share_ref[...])[:8]
        cw_ref[it, 0] = counted[:, :kids] + counted[:, kids:]

        def bufs(n):
            if n == 0:
                refs = (cw_ref, ci_ref, ci_ref, ci_ref, crr_ref, crl_ref, csr_ref, csl_ref)
                return [ref.at[it, 0] for ref in refs]
            refs = (w_ref, i_ref, j_ref, t_ref, rr_ref, rl_ref, sr_ref, sl_ref)
            return [ref.at[it, n - 1] for ref in refs]

        def swap(n):
            w, i = bufs(n)[:2]
            src = w.at[pl.ds(its_half, half_kids), :] if n else w
            return link(src, i, pair_send.at[it, 0, n], pair_recv.at[it, 0, n], (sibling, col))

        def swap_back(n):
            j, t = bufs(n)[2:4]
            return link(t, j, pair_send.at[it, 1, n], pair_recv.at[it, 1, n], (sibling, col))

        def shift_right(n, m):
            b = bufs(n)
            return link(b[6].at[m], b[4].at[m], chain_send.at[it, 0, n, m], chain_recv.at[it, 0, n, m], (ahead, col))

        def shift_left(n, m):
            b = bufs(n)
            return link(b[7].at[m], b[5].at[m], chain_send.at[it, 1, n, m], chain_recv.at[it, 1, n, m], (behind, col))

        def begin(n):
            swap(n).wait_recv()
            b = bufs(n)
            own = b[0][pl.ds(my_half, half_kids), :] if n else b[0][...]
            its = b[1][...]
            b[7][0] = jnp.where(is0, own + same * its, its + same * own)
            b[6][0] = jnp.where(is0, its + same * own, own + same * its)
            shift_right(n, 0).start()
            shift_left(n, 0).start()

        swap(0).start()
        for d in range(chunks):
            both = dot_nn(share_ref[...], xh_ref[d])
            rest = dot_nn(share_ref[:kids, :], xl_ref[d])
            w_ref[it, d] = both[:kids] + both[kids:] + rest
            swap(d + 1).start()
            begin(d)
        begin(chunks)
        for m in range(ROUNDS - 1):
            for n in range(chunks + 1):
                b = bufs(n)
                shift_right(n, m).wait_recv()
                b[6][m + 1] = b[6][0] + through_left * b[4][m]
                shift_right(n, m + 1).start()
                shift_left(n, m).wait_recv()
                b[7][m + 1] = b[7][0] + through_right * b[5][m]
                shift_left(n, m + 1).start()
        for n in range(chunks + 1):
            b = bufs(n)
            shift_right(n, ROUNDS - 1).wait_recv()
            shift_left(n, ROUNDS - 1).wait_recv()
            from_l, from_r = b[4][ROUNDS - 1], b[5][ROUNDS - 1]
            toward0, toward1 = b[7][0], b[6][0]
            if n == 0:
                count = jnp.where(is0, toward0, toward1) + mine_left * from_l + mine_right * from_r
                continue
            b[3][...] = jnp.where(is0, toward1, toward0) + other_left * from_l + other_right * from_r
            swap_back(n).start()
            b[0][pl.ds(my_half, half_kids), :] = (
                jnp.where(is0, toward0, toward1) + mine_left * from_l + mine_right * from_r
            )
        swap(0).wait_send()
        shrink = 1.0 / (jnp.broadcast_to(count[0:1, :], (kids, kids)).T + 1.0)
        shrink = jnp.concatenate([shrink] * (CHUNK // kids), axis=1)
        source = cent_ref if it == 0 else out_ref
        half_norm = jnp.zeros((kids, 1), F32)
        for d in range(chunks):
            swap(d + 1).wait_send()
            swap_back(d + 1).wait_recv()
            w_ref[it, d, pl.ds(its_half, half_kids), :] = j_ref[it, d]
            at = slice(d * CHUNK, (d + 1) * CHUNK)
            now = (w_ref[it, d] + source[:, at]) * shrink
            out_ref[:, at] = now
            if it + 1 < ITERS:
                encode(d, now)
                half_norm = half_norm + 0.5 * jnp.sum(now * now, axis=1, keepdims=True)
                for lo, size in spans:
                    scored = score(d, lo, size)
                    if d > 0:
                        scored = scored + logit_ref[:, lo : lo + size]
                    logit_ref[:, lo : lo + size] = scored
                    if d == chunks - 1:
                        summarize(it + 1, lo, size, half_norm)
        for n in range(chunks + 1):
            if n:
                swap_back(n).wait_send()
            for m in range(ROUNDS):
                shift_right(n, m).wait_send()
                shift_left(n, m).wait_send()

    for k in range(parts):
        for n in range(2):
            to_right(k, col, n).wait_send()
            to_left(k, col, n).wait_send()
        on_right(k, left).wait_send()
        on_left(k, right).wait_send()
        sent = moved(k)
        link(sent, sent, send_sem.at[k], recv_sem.at[k], (me, right)).wait_send()


def on_device(points, labels, boundaries, centroids):
    groups = lax.axis_size("grp")
    cols = lax.axis_size("col")
    rows, width = points.shape
    kids = centroids.shape[1]
    tile = width // LANES
    side = plane_side(groups)
    parts = side + 1
    seat_count = groups * SEATS
    all_rows = cols * seat_count
    chunks = width // CHUNK
    dma = pltpu.SemaphoreType.DMA
    vmem = pl.BlockSpec(memory_space=pltpu.VMEM)
    in_hbm = pl.BlockSpec(memory_space=pl.ANY)

    half = kids // 2
    one = pltpu.VMEM((ITERS, chunks, half, CHUNK), F32)
    many = pltpu.VMEM((ITERS, chunks, ROUNDS, half, CHUNK), F32)
    few = pltpu.VMEM((ITERS, 1, 8, kids), F32)
    few_rounds = pltpu.VMEM((ITERS, 1, ROUNDS, 8, kids), F32)

    out = pl.pallas_call(
        functools.partial(kernel, groups, cols),
        out_shape=jax.ShapeDtypeStruct((kids, width), F32),
        in_specs=[pl.BlockSpec(memory_space=pltpu.SMEM), vmem, in_hbm, in_hbm],
        out_specs=vmem,
        scratch_shapes=[
            pltpu.VMEM((rows, width), F32),
            pltpu.VMEM((kids, width), F32),
            pltpu.VMEM((seat_count * tile + tile, LANES), F32),
            pltpu.VMEM((cols, part_steps(parts - 1, side) * SEATS * tile, LANES), F32),
            pltpu.VMEM((all_rows * tile + tile, LANES), F32),
            pltpu.VMEM((chunks, all_rows, CHUNK), BF16),
            pltpu.VMEM((chunks, all_rows, CHUNK), BF16),
            pltpu.VMEM((kids, all_rows), F32),
            pltpu.VMEM((1, all_rows), F32),
            pltpu.VMEM((2 * kids, all_rows), BF16),
            pltpu.VMEM((chunks, 2 * kids, CHUNK), BF16),
            pltpu.VMEM((ITERS, 4, 2, all_rows), F32),
            pltpu.VMEM((ITERS, chunks, kids, CHUNK), F32), one, one, one, many, many, many, many,
            few, few, few_rounds, few_rounds, few_rounds, few_rounds,
            dma((parts,)), dma((parts,)), dma((3,)), dma((2, 2, parts)), dma((2, parts)), dma((2, parts)),
            dma((2, parts)), dma((2, parts)),
            pltpu.SemaphoreType.REGULAR,
            dma((ITERS, 3)), dma((ITERS, 3)),
            dma((ITERS, 2, chunks + 1)), dma((ITERS, 2, chunks + 1)),
            dma((ITERS, 2, chunks + 1, ROUNDS)), dma((ITERS, 2, chunks + 1, ROUNDS)),
        ],
        compiler_params=pltpu.CompilerParams(
            collective_id=0, has_side_effects=True, vmem_limit_bytes=56 << 20
        ),
    )(boundaries, labels.reshape(1, rows), points, centroids[0])
    return out[None]


def solution(mesh):
    placed = (P(("grp", "col"), None), P(("grp", "col")), P(), P("grp", "col", None))
    return jax.shard_map(
        on_device, mesh=mesh, in_specs=placed, out_specs=P("grp", "col", None), check_vma=False
    )
```
